32 devices in a mesh: groups: 1, chan: 16 (over z, y, x), grow: 2 (over core).
Axes of the slice: x: 2, y: 2, z: 4, core: 2. Of those that a mesh axis runs over, the one named last changes fastest.
Arguments:
- pair_input: bfloat16 [768, 768, 128], P(('groups', 'chan'), 'grow'), may hold values from -6 to 6
- token_mask: int32 [768], P('groups'), may hold values 0 or 1
- norm_gain: float32 [128], replicated, may hold values from 0.1 to 1.9
- left_gate: bfloat16 [128, 128], replicated, may hold values from -0.5 to 0.5
- left_value: bfloat16 [128, 128], replicated, may hold values from -0.5 to 0.5
- right_gate: bfloat16 [128, 128], replicated, may hold values from -0.5 to 0.5
- right_value: bfloat16 [128, 128], replicated, may hold values from -0.5 to 0.5
- sum_gain: float32 [128], replicated, may hold values from 0.1 to 1.9
- out_gate: bfloat16 [128, 128], replicated, may hold values from -0.5 to 0.5
- out_proj: bfloat16 [128, 128], replicated, may hold values from -0.5 to 0.5
Outputs:
- update: bfloat16 [768, 768, 128], P(('groups', 'chan'), 'grow')
The draws below stay inside these ranges and needn't reach their ends.
All inputs are finite; a program needn't handle non-finite values.
Results may differ from the reference program's by a relative error of at most 0.0083.
Values may be sent and summed in bfloat16 or wider, within the bound.
No kernel may reach another device: no remote copies, remote signals or barrier semaphores. Data moves between devices by JAX's collectives and lax.ppermute only.
A program may use at most 128 MiB of HBM per device.

```python
import jax
import jax.numpy as jnp
from jax import lax

C = 128
H = 128
N = 768


def plant(result, rng, smallest, top_value):
    place = [jax.random.randint(jax.random.fold_in(rng, axis), (), 0, length) for axis, length in enumerate(result.shape)]
    widest = result.shape.index(max(result.shape))
    neighbour = place[:widest] + [(place[widest] + 1) % result.shape[widest]] + place[widest + 1:]
    return result.at[tuple(place)].set(smallest).at[tuple(neighbour)].set(top_value)


def steps_of(own_key, extent, split, least, top_value):
    loudness = 1.0
    for axis_at, parts in split:
        heights = jax.random.uniform(jax.random.fold_in(jax.random.fold_in(own_key, 6), axis_at), (parts,), jnp.float32, least / len(split), top_value / len(split))
        loudness = loudness * jnp.repeat(jnp.exp(heights), extent[axis_at] // parts).reshape((-1,) + (1,) * (len(extent) - 1 - axis_at))
    return loudness


def gaussian(own_key, dims, width, reach, cuts=(), dtype=jnp.bfloat16):
    array = width * jax.random.normal(own_key, dims, jnp.float32)
    if cuts:
        array = array * steps_of(own_key, dims, cuts, -0.22, 0.18)
    return jnp.clip(array, -reach, reach).astype(dtype)


def setup_inputs(seed: int = 0, part: int = 0) -> dict:
    splits = jax.random.split(jax.random.key(seed), 11)
    own_keys = jax.random.split(jax.random.fold_in(splits[10], part), 11)
    pair_input = gaussian(own_keys[0], (N, N, C), 1.0, 6.0, ((0, 16), (1, 2)))
    token_mask = plant((jax.random.randint(own_keys[1], (N,), 0, 8) < 7).astype(jnp.int32), jax.random.fold_in(own_keys[1], 1), 0, 1)
    norm_gain = jnp.clip(1.0 + 0.18 * jax.random.normal(splits[2], (C,), jnp.float32), 0.1, 1.9)
    left_gate = gaussian(splits[3], (C, H), C ** -0.5, 0.5)
    left_value = gaussian(splits[4], (C, H), C ** -0.5, 0.5)
    right_gate = gaussian(splits[5], (C, H), C ** -0.5, 0.5)
    right_value = gaussian(splits[6], (C, H), C ** -0.5, 0.5)
    sum_gain = jnp.clip(1.0 + 0.18 * jax.random.normal(splits[7], (H,), jnp.float32), 0.1, 1.9)
    out_gate = gaussian(splits[8], (C, C), C ** -0.5, 0.5)
    out_proj = gaussian(splits[9], (H, C), H ** -0.5, 0.5)
    return dict(pair_input=pair_input, token_mask=token_mask, norm_gain=norm_gain, left_gate=left_gate, left_value=left_value, right_gate=right_gate, right_value=right_value, sum_gain=sum_gain, out_gate=out_gate, out_proj=out_proj)


norm_eps = 1e-05

def layer_norm(values, gain_vec, along_axis):
    average = lax.optimization_barrier(jnp.mean(values, axis=along_axis, keepdims=True))
    centred = values - average
    spread = lax.optimization_barrier(jnp.mean(centred * centred, axis=along_axis, keepdims=True))
    return centred * lax.rsqrt(spread + norm_eps) * gain_vec

def reference(pair_input, token_mask, norm_gain, left_gate, left_value, right_gate, right_value, sum_gain, out_gate, out_proj):
    normed = layer_norm(pair_input.astype(jnp.float32), norm_gain, -1).astype(jnp.bfloat16)
    flat = normed.reshape(N * N, C)

    def project(weight):
        return jnp.dot(flat, weight, preferred_element_type=jnp.float32).reshape(N, N, -1)
    valid = token_mask.astype(jnp.float32)
    pair_mask = (valid[:, None] * valid[None, :])[:, :, None]
    left_op = (jax.nn.sigmoid(project(left_gate)) * project(left_value) * pair_mask).astype(jnp.bfloat16)
    right_op = (jax.nn.sigmoid(project(right_gate)) * project(right_value) * pair_mask).astype(jnp.bfloat16)
    left_op = jnp.transpose(left_op, (2, 0, 1))
    right_op = jnp.transpose(right_op, (2, 0, 1))

    def contract(operands):
        return jnp.dot(operands[0], operands[1].T, preferred_element_type=jnp.float32).astype(jnp.bfloat16)
    contracted = lax.map(contract, (left_op, right_op))
    mixed_out = layer_norm(contracted.astype(jnp.float32), sum_gain[:, None, None], 0).astype(jnp.bfloat16)
    mixed_flat = jnp.transpose(mixed_out, (1, 2, 0)).reshape(N * N, H)
    linear = jnp.dot(mixed_flat, out_proj, preferred_element_type=jnp.float32)
    gate_act = jax.nn.sigmoid(jnp.dot(flat, out_gate, preferred_element_type=jnp.float32))
    return (gate_act * linear).reshape(N, N, C).astype(jnp.bfloat16)
```

```python
import functools
import jax
import jax.numpy as jnp
from jax import lax
from jax.experimental import pallas as pl
from jax.experimental.pallas import tpu as pltpu
from jax.sharding import Mesh
from jax.sharding import PartitionSpec as P

norm_eps = 1e-05
ROWS = 16
LANES = 128
VMEM_BYTES = 56 * 1024 * 1024


def params(**kw):
    return pltpu.CompilerParams(vmem_limit_bytes=VMEM_BYTES, **kw)


def sigmoid(x):
    return 1.0 / (1.0 + jnp.exp(-x))


def project_kernel(sizes, owners, hidden, norm_first, row_ref, col_ref, x_ref, w_ref, gain_ref, *refs):
    if norm_first:
        normed_ref, *outs, held = refs
    else:
        *outs, held = refs
    at = pl.program_id(0) * ROWS

    def one_row(i, _):
        if norm_first:
            x = x_ref[i].astype(jnp.float32)
            centred = x - jnp.mean(x, axis=-1, keepdims=True)
            spread = jnp.mean(centred * centred, axis=-1, keepdims=True)
            normed = (centred * lax.rsqrt(spread + norm_eps) * gain_ref[...]).astype(jnp.bfloat16)
            normed_ref[i] = normed
        else:
            normed = x_ref[i]
        both = lax.dot_general(
            w_ref[...], normed, (((1,), (1,)), ((), ())), preferred_element_type=jnp.float32
        )
        valid = col_ref[...] * row_ref[at + i]
        gated = sigmoid(both[:hidden]) * both[hidden:] * valid
        for j in range(held.shape[0]):
            held[j, pl.ds(pl.multiple_of(i * hidden, hidden), hidden), :] = gated[:, j * LANES:(j + 1) * LANES]
        return 0

    lax.fori_loop(0, ROWS, one_row, 0, unroll=2)
    offset = 0
    for out, size in zip(outs, sizes):
        def one_owner(d, _, out=out, size=size, offset=offset):
            for e in range(size):
                channel = offset * owners + d * size + e
                for j in range(held.shape[0]):
                    out[d, e, :, j * LANES:(j + 1) * LANES] = held[j, pl.ds(channel, ROWS, stride=hidden), :].astype(jnp.bfloat16)
            return 0
        lax.fori_loop(0, owners, one_owner, 0, unroll=2)
        offset += size


def project(x, gate, value, gain, row_valid, col_valid, sizes, owners, norm_first):
    rows, cols, width = x.shape
    hidden = gate.shape[1]
    w = jnp.concatenate([gate, value], axis=1).T
    out_shape = [jax.ShapeDtypeStruct((owners, s, rows, cols), jnp.bfloat16) for s in sizes]
    out_specs = [pl.BlockSpec((owners, s, ROWS, cols), lambda r: (0, 0, r, 0)) for s in sizes]
    x_spec = pl.BlockSpec((ROWS, cols, width), lambda r: (r, 0, 0))
    if norm_first:
        out_shape = [jax.ShapeDtypeStruct(x.shape, jnp.bfloat16)] + out_shape
        out_specs = [x_spec] + out_specs
    whole = lambda shape: pl.BlockSpec(shape, lambda r: (0,) * len(shape))
    return pl.pallas_call(
        functools.partial(project_kernel, sizes, owners, hidden, norm_first),
        grid=(rows // ROWS,),
        in_specs=[
            pl.BlockSpec(memory_space=pltpu.SMEM),
            whole((1, cols)),
            x_spec,
            whole(w.shape),
            whole((1, width)),
        ],
        out_specs=out_specs,
        out_shape=out_shape,
        scratch_shapes=[pltpu.VMEM((cols // LANES, ROWS * hidden, LANES), jnp.float32)],
        compiler_params=params(),
        name="project",
    )(row_valid, col_valid[None], x, w, gain[None])


def contract_kernel(n_left, n_right, rows, cols, place_ref, *refs):
    lefts, rights = refs[:n_left], refs[n_left:n_left + n_right]
    outs = refs[n_left + n_right:2 * n_left + n_right]
    left_all, right_all = refs[2 * n_left + n_right:]
    for s, right in enumerate(rights):
        base = place_ref[s] * (4 * rows)
        for b in range(4):
            for k in range(2):
                right_all[pl.ds(pl.multiple_of(base + b * rows, rows), rows), k * cols:(k + 1) * cols] = right[2 * b + k, 0]
    for s, left in enumerate(lefts):
        for b in range(4):
            for k in range(2):
                left_all[(s * 4 + b) * rows:(s * 4 + b + 1) * rows, k * cols:(k + 1) * cols] = left[2 * b + k, 0]
    for k in range(2):
        total = lax.dot_general(
            left_all[...], right_all[k * cols:(k + 1) * cols, :], (((1,), (1,)), ((), ())),
            preferred_element_type=jnp.float32,
        ).astype(jnp.bfloat16)
        for s, out in enumerate(outs):
            for b in range(4):
                out[2 * b + k, 0] = total[(s * 4 + b) * rows:(s * 4 + b + 1) * rows]


def contract(lefts, rights, place):
    size, rows, cols = lefts[0][0].shape[1:]
    spec = lambda at: pl.BlockSpec((8, 1, rows, cols), lambda q, at=at: (at, q, 0, 0))
    blocks = [*lefts, *rights]
    return pl.pallas_call(
        functools.partial(contract_kernel, len(lefts), len(rights), rows, cols),
        grid=(size,),
        in_specs=[pl.BlockSpec(memory_space=pltpu.SMEM)] + [spec(at) for _, at in blocks],
        out_specs=[spec(0) for _ in lefts],
        out_shape=[jax.ShapeDtypeStruct((8, size, rows, cols), jnp.bfloat16) for _ in lefts],
        scratch_shapes=[
            pltpu.VMEM((len(lefts) * 4 * rows, 2 * cols), jnp.bfloat16),
            pltpu.VMEM((len(rights) * 4 * rows, 2 * cols), jnp.bfloat16),
        ],
        compiler_params=params(),
        name="contract",
    )(place, *[a for a, _ in blocks])


def finish_kernel(n, gain_ref, normed_ref, proj_ref, gate_ref, *refs):
    chunks, out_ref, held = refs[:n], refs[n], refs[n + 1]
    channels = sum(c.shape[0] for c in chunks)
    rows, cols = chunks[0].shape[1:]
    total = jnp.zeros((rows, cols), jnp.float32)
    for c in chunks:
        total = total + jnp.sum(c[...].astype(jnp.float32), axis=0)
    average = total * (1.0 / channels)
    spread = jnp.zeros((rows, cols), jnp.float32)
    for c in chunks:
        centred = c[...].astype(jnp.float32) - average
        spread = spread + jnp.sum(centred * centred, axis=0)
    scale = lax.rsqrt(spread * (1.0 / channels) + norm_eps)
    at = 0
    for c in chunks:
        for h in range(c.shape[0]):
            mixed = (c[h].astype(jnp.float32) - average) * scale * gain_ref[at + h]
            for j in range(held.shape[0]):
                held[j, (at + h) * rows:(at + h + 1) * rows, :] = mixed[:, j * LANES:(j + 1) * LANES]
        at += c.shape[0]

    def one_row(i, _):
        mixed = jnp.concatenate([held[j, pl.ds(i, channels, stride=rows), :] for j in range(held.shape[0])], axis=1).astype(jnp.bfloat16)
        linear = lax.dot_general(mixed, proj_ref[...], (((0,), (0,)), ((), ())), preferred_element_type=jnp.float32)
        gate = jnp.dot(normed_ref[i], gate_ref[...], preferred_element_type=jnp.float32)
        out_ref[i] = (sigmoid(gate) * linear).astype(jnp.bfloat16)
        return 0

    lax.fori_loop(0, rows, one_row, 0, unroll=2)


def finish(chunks, normed, gain, proj, out_gate):
    rows, cols, width = normed.shape
    channels = sum(c.shape[0] for c in chunks)
    block = pl.BlockSpec((ROWS, cols, width), lambda r: (r, 0, 0))
    whole = lambda shape: pl.BlockSpec(shape, lambda r: (0,) * len(shape))
    return pl.pallas_call(
        functools.partial(finish_kernel, len(chunks)),
        grid=(rows // ROWS,),
        in_specs=[pl.BlockSpec(memory_space=pltpu.SMEM), block, whole(proj.shape), whole(out_gate.shape)]
        + [pl.BlockSpec((c.shape[0], ROWS, cols), lambda r: (0, r, 0)) for c in chunks],
        out_specs=block,
        out_shape=jax.ShapeDtypeStruct(normed.shape, jnp.bfloat16),
        scratch_shapes=[pltpu.VMEM((cols // LANES, channels * ROWS, LANES), jnp.float32)],
        compiler_params=params(),
        name="finish",
    )(gain, normed, proj, out_gate, *chunks)

ALL = ("z", "y", "x", "core")


def exchange(x, axes):
    return lax.all_to_all(x, axes, split_axis=0, concat_axis=0, tiled=True)


def per_device(
    pair_input, token_mask, norm_gain, left_gate, left_value, right_gate, right_value, sum_gain, out_gate, out_proj
):
    rows, cols, _ = pair_input.shape
    hidden = left_gate.shape[1]
    chip = lax.axis_index(("z", "y", "x"))
    valid = token_mask.astype(jnp.float32)
    row_valid = lax.dynamic_slice_in_dim(valid, chip * rows, rows, 0)
    col_valid = lax.dynamic_slice_in_dim(valid, lax.axis_index("core") * cols, cols, 0)
    owners = lax.axis_size(ALL)
    sizes = (hidden // owners,)
    planes = lax.axis_size("z")
    place = jnp.arange(planes, dtype=jnp.int32)
    normed, right = project(
        pair_input, right_gate, right_value, norm_gain, row_valid, col_valid, sizes, owners, True
    )
    right = exchange(right, ALL)
    (left,) = project(normed, left_gate, left_value, norm_gain, row_valid, col_valid, sizes, owners, False)
    left = exchange(left, ALL)
    outs = contract([(left, p) for p in range(planes)], [(right, p) for p in range(planes)], place)
    returned = exchange(jnp.concatenate(outs), ALL)
    returned = returned.reshape(hidden, rows, cols)
    return finish([returned], normed, sum_gain, out_proj, out_gate)


def solution(mesh):
    grid = mesh.devices
    fine = Mesh(
        grid.reshape(grid.shape[0], grid.shape[1] // 4, 2, 2, grid.shape[2]), ("groups", "z", "y", "x", "core")
    )
    pair = P(("groups", "z", "y", "x"), "core", None)
    return jax.shard_map(
        per_device, mesh=fine, in_specs=(pair, P("groups")) + (P(),) * 8, out_specs=pair, check_vma=False
    )
```

```python
import functools

import jax
import jax.numpy as jnp
from jax import lax
from jax.experimental import pallas as pl
from jax.experimental.pallas import tpu as pltpu
from jax.sharding import Mesh
from jax.sharding import PartitionSpec as P

norm_eps = 1e-05
ROWS = 16
LANES = 128
VMEM_BYTES = 56 * 1024 * 1024
HALF = ("near", "y", "x", "core")
ALL = ("half", *HALF)
SPLIT = (5, 3)


def params():
    return pltpu.CompilerParams(vmem_limit_bytes=VMEM_BYTES)


def sigmoid(x):
    grown = 1.0 + jnp.exp(-jnp.maximum(x, -80.0))
    guess = pl.reciprocal(grown, approx=True)
    return guess * (2.0 - grown * guess)


def spec_whole(shape):
    return pl.BlockSpec(shape, lambda r: (0,) * len(shape))


SMEM = pl.BlockSpec(memory_space=pltpu.SMEM)


def project_kernel(low, high, norm_first, write, mask_ref, col_ref, at_ref, x_ref, gate_ref, value_ref, gain_ref, *refs):
    *outs, held, w_ref = refs
    count = high - low
    step = pl.program_id(0)

    @pl.when(step == 0)
    def _():
        w_ref[:count] = gate_ref[...].astype(jnp.float32).T[low:high].astype(jnp.bfloat16)
        w_ref[count:] = value_ref[...].astype(jnp.float32).T[low:high].astype(jnp.bfloat16)

    first_row = at_ref[0] + step * ROWS
    col_valid = col_ref[at_ref[1]].astype(jnp.float32)
    if norm_first:
        normed_ref, *outs = outs

    def one_row(i, _):
        if norm_first:
            x = x_ref[i].astype(jnp.float32)
            centred = x - jnp.mean(x, axis=-1, keepdims=True)
            spread = jnp.mean(centred * centred, axis=-1, keepdims=True)
            normed = (centred * lax.rsqrt(spread + norm_eps) * gain_ref[...]).astype(jnp.bfloat16)
            normed_ref[i] = normed
        else:
            normed = x_ref[i]
        both = lax.dot_general(w_ref[...], normed, (((1,), (1,)), ((), ())), preferred_element_type=jnp.float32)
        valid = col_valid * mask_ref[first_row + i].astype(jnp.float32)
        gated = sigmoid(both[:count]) * both[count:] * valid
        for j in range(held.shape[0]):
            held[j, pl.ds(pl.multiple_of(i * count, 8), count), :] = gated[:, j * LANES:(j + 1) * LANES]
        return 0

    lax.fori_loop(0, ROWS, one_row, 0, unroll=2)

    def channel(j, c):
        return held[j, pl.ds(c, ROWS, stride=count), :].astype(jnp.bfloat16)

    write(outs, channel, at_ref)


def write_right(size, owners, outs, channel, at_ref):
    (out,) = outs

    def one_owner(o, _):
        for e in range(size):
            for j in range(out.shape[-1] // LANES):
                block = channel(j, o * size + e)
                for h in range(2):
                    out[h * owners + o, e, :, j * LANES:(j + 1) * LANES] = block
        return 0

    lax.fori_loop(0, owners, one_owner, 0, unroll=2)


def write_left(sizes, owners, outs, channel, at_ref):
    for d, out in enumerate(outs):
        owner = at_ref[2] ^ d
        first = 0
        for size in sizes:
            for e in range(size):
                for j in range(out.shape[-1] // LANES):
                    out[first + e, :, j * LANES:(j + 1) * LANES] = channel(j, first * owners + owner * size + e)
            first += size


def project(x, gate, value, gain, mask, col_mask, at, low, high, norm_first, write, out_blocks):
    rows, cols, width = x.shape
    count = high - low
    x_spec = pl.BlockSpec((ROWS, cols, width), lambda r: (r, 0, 0))
    out_shape = [jax.ShapeDtypeStruct((*lead, rows, cols), jnp.bfloat16) for lead in out_blocks]
    out_specs = [pl.BlockSpec((*lead, ROWS, cols), lambda r, n=len(lead): (0,) * n + (r, 0)) for lead in out_blocks]
    if norm_first:
        out_shape = [jax.ShapeDtypeStruct(x.shape, jnp.bfloat16), *out_shape]
        out_specs = [x_spec, *out_specs]
    return pl.pallas_call(
        functools.partial(project_kernel, low, high, norm_first, write),
        grid=(rows // ROWS,),
        in_specs=[SMEM, spec_whole(col_mask.shape), SMEM, x_spec]
        + [spec_whole(gate.shape)] * 2 + [spec_whole((1, width))],
        out_specs=out_specs,
        out_shape=out_shape,
        scratch_shapes=[
            pltpu.VMEM((cols // LANES, ROWS * count, LANES), jnp.float32),
            pltpu.VMEM((2 * count, width), jnp.bfloat16),
        ],
        compiler_params=params(),
        cost_estimate=pl.CostEstimate(
            flops=4 * rows * cols * width * count, bytes_accessed=8 * rows * cols * width, transcendentals=rows * cols * count
        ),
        name="project",
    )(mask, col_mask, at, x, gate, value, gain[None])


def contract_kernel(n, by_partner, rows, cols, at_ref, *refs):
    lefts, right = refs[:n], refs[n]
    outs = refs[n + 1:-3]
    left_all, right_all, sums = refs[-3:]
    for s in range(right.shape[0]):
        right_all[s % 2, (s // 2) * rows:(s // 2 + 1) * rows, :] = right[s, 0]
    for d, left in enumerate(lefts):
        source = at_ref[2] ^ d
        left_all[source & 1, pl.ds(pl.multiple_of((source >> 1) * rows, rows), rows), :] = left[0]
    dims = (((1,), (1,)), ((), ()))
    for k in range(2):
        total = sum(
            lax.dot_general(left_all[p], right_all[p, k * cols:(k + 1) * cols, :], dims, preferred_element_type=jnp.float32)
            for p in range(2)
        ).astype(jnp.bfloat16)
        if by_partner:
            sums[k] = total
        else:
            for b in range(n // 2):
                outs[0][2 * b + k, 0] = total[b * rows:(b + 1) * rows]
    if by_partner:
        for d, out in enumerate(outs):
            target = at_ref[2] ^ d
            out[0] = sums[target & 1, pl.ds(pl.multiple_of((target >> 1) * rows, rows), rows), :]


def contract(lefts, right, at, first, by_partner):
    everyone, size, rows, cols = right.shape
    n = len(lefts)
    out_shape = [jax.ShapeDtypeStruct((size, rows, cols), jnp.bfloat16)] * n
    out_specs = [pl.BlockSpec((1, rows, cols), lambda q: (q, 0, 0))] * n
    if not by_partner:
        out_shape = [jax.ShapeDtypeStruct((n, size, rows, cols), jnp.bfloat16)]
        out_specs = [pl.BlockSpec((n, 1, rows, cols), lambda q: (0, q, 0, 0))]
    return pl.pallas_call(
        functools.partial(contract_kernel, n, by_partner, rows, cols),
        grid=(size,),
        in_specs=[SMEM]
        + [pl.BlockSpec((1, rows, cols), lambda q: (first + q, 0, 0))] * n
        + [pl.BlockSpec((everyone, 1, rows, cols), lambda q: (0, q, 0, 0))],
        out_specs=out_specs,
        out_shape=out_shape,
        scratch_shapes=[
            pltpu.VMEM((2, n // 2 * rows, cols), jnp.bfloat16),
            pltpu.VMEM((2, everyone // 2 * rows, cols), jnp.bfloat16),
            pltpu.VMEM((2, n // 2 * rows, cols), jnp.bfloat16),
        ],
        compiler_params=params(),
        cost_estimate=pl.CostEstimate(
            flops=size * 2 * n * n * everyone // 4 * rows * rows * cols,
            bytes_accessed=size * (everyone + 2 * n) * rows * cols * 2,
            transcendentals=0,
        ),
        name="contract",
    )(at, *lefts, right)


def finish_kernel(plan, at_ref, gain_ref, normed_ref, proj_ref, gate_ref, *refs):
    blocks, out_ref, held = refs[:len(plan)], refs[-2], refs[-1]
    rows, cols = normed_ref.shape[:2]
    pieces = []
    for block, (first, size, partner) in zip(blocks, plan):
        if partner is None:
            pieces += [(block.at[o, e], first + o * size + e) for o in range(block.shape[0]) for e in range(size)]
        else:
            base = first + (at_ref[2] ^ partner) * size
            pieces += [(block.at[e], base + e) for e in range(size)]
    channels = len(pieces)
    total = jnp.zeros((rows, cols), jnp.float32)
    for piece, _ in pieces:
        total = total + piece[...].astype(jnp.float32)
    average = total * (1.0 / channels)
    spread = jnp.zeros((rows, cols), jnp.float32)
    for piece, _ in pieces:
        centred = piece[...].astype(jnp.float32) - average
        spread = spread + centred * centred
    scale = lax.rsqrt(spread * (1.0 / channels) + norm_eps)
    for piece, c in pieces:
        mixed = (piece[...].astype(jnp.float32) - average) * scale * gain_ref[c]
        for j in range(held.shape[0]):
            held[j, pl.ds(pl.multiple_of(c * rows, rows), rows), :] = mixed[:, j * LANES:(j + 1) * LANES]

    def one_row(i, _):
        mixed = jnp.concatenate(
            [held[j, pl.ds(i, channels, stride=rows), :] for j in range(held.shape[0])], axis=1
        ).astype(jnp.bfloat16)
        linear = lax.dot_general(mixed, proj_ref[...], (((0,), (0,)), ((), ())), preferred_element_type=jnp.float32)
        gate = jnp.dot(normed_ref[i], gate_ref[...], preferred_element_type=jnp.float32)
        out_ref[i] = (sigmoid(gate) * linear).astype(jnp.bfloat16)
        return 0

    lax.fori_loop(0, rows, one_row, 0, unroll=2)


def finish(blocks, plan, at, normed, gain, proj, out_gate):
    rows, cols, width = normed.shape
    pair = pl.BlockSpec((ROWS, cols, width), lambda r: (r, 0, 0))
    return pl.pallas_call(
        functools.partial(finish_kernel, plan),
        grid=(rows // ROWS,),
        in_specs=[SMEM, SMEM, pair, spec_whole(proj.shape), spec_whole(out_gate.shape)]
        + [pl.BlockSpec((*b.shape[:-2], ROWS, cols), lambda r, n=b.ndim - 2: (0,) * n + (r, 0)) for b in blocks],
        out_specs=pair,
        out_shape=jax.ShapeDtypeStruct(normed.shape, jnp.bfloat16),
        scratch_shapes=[pltpu.VMEM((cols // LANES, proj.shape[0] * ROWS, LANES), jnp.float32)],
        compiler_params=params(),
        name="finish",
    )(at, gain, normed, proj, out_gate, *blocks)


def exchange(x, axes):
    return lax.all_to_all(x, axes, split_axis=0, concat_axis=0, tiled=True)


def partners(blocks):
    n = len(blocks)
    return [blocks[0]] + [lax.ppermute(blocks[d], HALF, [(i, i ^ d) for i in range(n)]) for d in range(1, n)]


def after(x, *others):
    return lax.optimization_barrier((x, *others))[0]


def per_device(
    pair_input, token_mask, norm_gain, left_gate, left_value, right_gate, right_value, sum_gain, out_gate, out_proj
):
    rows, cols, _ = pair_input.shape
    hidden = left_gate.shape[1]
    owners = lax.axis_size(HALF)
    chip = lax.axis_index(("half", "near", "y", "x"))
    at = jnp.stack([chip * rows, lax.axis_index("core"), lax.axis_index(HALF)]).astype(jnp.int32)
    col_mask = token_mask.reshape(-1, 1, cols)
    own = hidden // owners
    share = own // sum(SPLIT)
    sizes = tuple(s * share for s in SPLIT)
    firsts = tuple(sum(sizes[:q]) for q in range(len(sizes)))

    def right_chunk(x, q, norm_first):
        return project(
            x, right_gate, right_value, norm_gain, token_mask, col_mask, at,
            firsts[q] * owners, (firsts[q] + sizes[q]) * owners, norm_first,
            functools.partial(write_right, sizes[q], owners), [(2 * owners, sizes[q])],
        )

    normed, right = right_chunk(pair_input, 0, True)
    rights = [exchange(right, ALL)]
    lefts = project(
        normed, left_gate, left_value, norm_gain, token_mask, col_mask, at, 0, hidden, False,
        functools.partial(write_left, sizes, owners), [(own,)] * owners,
    )
    lefts = partners(lefts)
    for q in range(1, len(sizes)):
        (right,) = right_chunk(normed, q, False)
        rights.append(exchange(after(right, rights[-1], *lefts), ALL))
    blocks, plan = [], []
    for q, size in enumerate(sizes):
        last = q == len(sizes) - 1
        outs = contract(lefts, rights[q] if q == 0 else after(rights[q], *blocks), at, firsts[q], not last)
        if last:
            blocks.append(exchange(outs[0], HALF))
            plan.append((firsts[q] * owners, size, None))
        else:
            blocks += partners(outs)
            plan += [(firsts[q] * owners, size, d) for d in range(owners)]
    return finish(blocks, tuple(plan), at, normed, sum_gain, out_proj, out_gate)


def solution(mesh):
    grid = mesh.devices
    fine = Mesh(
        grid.reshape(grid.shape[0], 2, grid.shape[1] // 8, 2, 2, grid.shape[2]), ("groups", *ALL)
    )
    pair = P(("groups", "half", "near", "y", "x"), "core", None)
    return jax.shard_map(
        per_device, mesh=fine, in_specs=(pair, P("groups")) + (P(),) * 8, out_specs=pair, check_vma=False
    )
```

```python
import functools

import jax
import jax.numpy as jnp
from jax import lax
from jax.experimental import pallas as pl
from jax.experimental.pallas import tpu as pltpu
from jax.sharding import Mesh
from jax.sharding import PartitionSpec as P

norm_eps = 1e-05
ROWS = 16
LANES = 128
VMEM_BYTES = 56 * 1024 * 1024
HALF = ("near", "y", "x", "core")
ALL = ("half", *HALF)
SPLIT = (5, 3)


def params():
    return pltpu.CompilerParams(vmem_limit_bytes=VMEM_BYTES)


def sigmoid(x):
    grown = 1.0 + jnp.exp(-jnp.maximum(x, -80.0))
    guess = pl.reciprocal(grown, approx=True)
    return guess * (2.0 - grown * guess)


def spec_whole(shape):
    return pl.BlockSpec(shape, lambda r: (0,) * len(shape))


SMEM = pl.BlockSpec(memory_space=pltpu.SMEM)


def project_kernel(low, high, norm_first, keep, write, mask_ref, at_ref, x_ref, gate_ref, value_ref, gain_ref, *refs):
    *outs, held, w_ref, gain_all = refs
    col_valid = 1.0
    if keep is not None:
        col_ref, *outs = outs
        col_valid = col_ref[at_ref[1]].astype(jnp.float32)
    count = high - low
    step = pl.program_id(0)

    @pl.when(step == 0)
    def _():
        w_ref[:count] = gate_ref[...].astype(jnp.float32).T[low:high].astype(jnp.bfloat16)
        w_ref[count:] = value_ref[...].astype(jnp.float32).T[low:high].astype(jnp.bfloat16)
        gain = jnp.broadcast_to(gain_ref[...], (gain_ref.shape[1], gain_ref.shape[1])).T
        gain_all[...] = jnp.broadcast_to(gain[:, :1], gain_all.shape)

    first_row = at_ref[0] + step * ROWS
    if keep:
        normed_ref, *outs = outs

    def one_row(i, _):
        if norm_first:
            x = x_ref[i].T.astype(jnp.float32)
            centred = x - jnp.mean(x, axis=0, keepdims=True)
            spread = jnp.mean(centred * centred, axis=0, keepdims=True)
            normed = (centred * lax.rsqrt(spread + norm_eps) * gain_all[...]).astype(jnp.bfloat16)
            if keep:
                normed_ref[i] = normed
        else:
            normed = x_ref[i]
        both = jnp.dot(w_ref[...], normed, preferred_element_type=jnp.float32)
        valid = mask_ref[first_row + i].astype(jnp.float32) * col_valid
        gated = sigmoid(both[:count]) * both[count:] * valid
        for j in range(held.shape[0]):
            held[j, pl.ds(pl.multiple_of(i * count, 8), count), :] = gated[:, j * LANES:(j + 1) * LANES]
        return 0

    lax.fori_loop(0, ROWS, one_row, 0, unroll=ROWS)

    def channel(j, c):
        return held[j, pl.ds(c, ROWS, stride=count), :].astype(jnp.bfloat16)

    write(outs, channel, at_ref)


def write_right(size, owners, outs, channel, at_ref):
    (out,) = outs

    def one_owner(o, _):
        for e in range(size):
            for j in range(out.shape[-1] // LANES):
                block = channel(j, o * size + e)
                for h in range(2):
                    out[h * owners + o, e, :, j * LANES:(j + 1) * LANES] = block
        return 0

    lax.fori_loop(0, owners, one_owner, 0, unroll=2)


def write_left(sizes, owners, outs, channel, at_ref):
    for d, out in enumerate(outs):
        owner = at_ref[2] ^ d
        first = 0
        for size in sizes:
            for e in range(size):
                for j in range(out.shape[-1] // LANES):
                    out[first + e, :, j * LANES:(j + 1) * LANES] = channel(j, first * owners + owner * size + e)
            first += size


def project(x, gate, value, gain, mask, col_mask, at, low, high, norm_first, keep, write, out_blocks):
    rows, cols, width = x.shape if norm_first else (x.shape[0], x.shape[2], x.shape[1])
    count = high - low
    x_spec = pl.BlockSpec((ROWS, *x.shape[1:]), lambda r: (r, 0, 0))
    out_shape = [jax.ShapeDtypeStruct((*lead, rows, cols), jnp.bfloat16) for lead in out_blocks]
    out_specs = [pl.BlockSpec((*lead, ROWS, cols), lambda r, n=len(lead): (0,) * n + (r, 0)) for lead in out_blocks]
    if keep:
        out_shape = [jax.ShapeDtypeStruct((rows, width, cols), jnp.bfloat16), *out_shape]
        out_specs = [pl.BlockSpec((ROWS, width, cols), lambda r: (r, 0, 0)), *out_specs]
    extra = [] if keep is None else [col_mask]
    return pl.pallas_call(
        functools.partial(project_kernel, low, high, norm_first, keep, write),
        grid=(rows // ROWS,),
        in_specs=[SMEM, SMEM, x_spec]
        + [spec_whole(gate.shape)] * 2 + [spec_whole((1, width))] + [spec_whole(e.shape) for e in extra],
        out_specs=out_specs,
        out_shape=out_shape,
        scratch_shapes=[
            pltpu.VMEM((cols // LANES, ROWS * count, LANES), jnp.float32),
            pltpu.VMEM((2 * count, width), jnp.bfloat16),
            pltpu.VMEM((width, cols), jnp.float32),
        ],
        compiler_params=params(),
        cost_estimate=pl.CostEstimate(
            flops=4 * rows * cols * width * count, bytes_accessed=8 * rows * cols * width, transcendentals=rows * cols * count
        ),
        name="project",
    )(mask, at, x, gate, value, gain[None], *extra)


def gate_kernel(normed_ref, gate_ref, out_ref):
    def one_row(i, _):
        gate = lax.dot_general(normed_ref[i], gate_ref[...], (((0,), (0,)), ((), ())), preferred_element_type=jnp.float32)
        out_ref[i] = sigmoid(gate).astype(out_ref.dtype)
        return 0

    lax.fori_loop(0, normed_ref.shape[0], one_row, 0, unroll=4)


def output_gate(normed, out_gate):
    rows, width, cols = normed.shape
    return pl.pallas_call(
        gate_kernel,
        grid=(rows // ROWS,),
        in_specs=[pl.BlockSpec((ROWS, width, cols), lambda r: (r, 0, 0)), spec_whole(out_gate.shape)],
        out_specs=pl.BlockSpec((ROWS, cols, width), lambda r: (r, 0, 0)),
        out_shape=jax.ShapeDtypeStruct((rows, cols, width), jnp.float32),
        compiler_params=params(),
        cost_estimate=pl.CostEstimate(
            flops=2 * rows * cols * width * width, bytes_accessed=4 * rows * cols * width, transcendentals=rows * cols * width
        ),
        name="output_gate",
    )(normed, out_gate)


def contract_kernel(n, by_partner, rows, cols, at_ref, *refs):
    lefts, right = refs[:n], refs[n]
    outs = refs[n + 1:-3]
    left_all, right_all, sums = refs[-3:]
    for s in range(right.shape[0]):
        right_all[s % 2, (s // 2) * rows:(s // 2 + 1) * rows, :] = right[s, 0]
    for d, left in enumerate(lefts):
        source = at_ref[2] ^ d
        left_all[source & 1, pl.ds(pl.multiple_of((source >> 1) * rows, rows), rows), :] = left[0]
    dims = (((1,), (1,)), ((), ()))
    for k in range(2):
        total = sum(
            lax.dot_general(left_all[p], right_all[p, k * cols:(k + 1) * cols, :], dims, preferred_element_type=jnp.float32)
            for p in range(2)
        ).astype(jnp.bfloat16)
        if by_partner:
            sums[k] = total
        else:
            for b in range(n // 2):
                outs[0][2 * b + k, 0] = total[b * rows:(b + 1) * rows]
    if by_partner:
        for d, out in enumerate(outs):
            target = at_ref[2] ^ d
            out[0] = sums[target & 1, pl.ds(pl.multiple_of((target >> 1) * rows, rows), rows), :]


def contract(lefts, right, at, first, by_partner):
    everyone, size, rows, cols = right.shape
    n = len(lefts)
    out_shape = [jax.ShapeDtypeStruct((size, rows, cols), jnp.bfloat16)] * n
    out_specs = [pl.BlockSpec((1, rows, cols), lambda q: (q, 0, 0))] * n
    if not by_partner:
        out_shape = [jax.ShapeDtypeStruct((n, size, rows, cols), jnp.bfloat16)]
        out_specs = [pl.BlockSpec((n, 1, rows, cols), lambda q: (0, q, 0, 0))]
    return pl.pallas_call(
        functools.partial(contract_kernel, n, by_partner, rows, cols),
        grid=(size,),
        in_specs=[SMEM]
        + [pl.BlockSpec((1, rows, cols), lambda q: (first + q, 0, 0))] * n
        + [pl.BlockSpec((everyone, 1, rows, cols), lambda q: (0, q, 0, 0))],
        out_specs=out_specs,
        out_shape=out_shape,
        scratch_shapes=[
            pltpu.VMEM((2, n // 2 * rows, cols), jnp.bfloat16),
            pltpu.VMEM((2, everyone // 2 * rows, cols), jnp.bfloat16),
            pltpu.VMEM((2, n // 2 * rows, cols), jnp.bfloat16),
        ],
        compiler_params=params(),
        cost_estimate=pl.CostEstimate(
            flops=size * 2 * n * n * everyone // 4 * rows * rows * cols,
            bytes_accessed=size * (everyone + 2 * n) * rows * cols * 2,
            transcendentals=0,
        ),
        name="contract",
    )(at, *lefts, right)


def gather_kernel(size, at_ref, *refs):
    blocks, turned_ref, stats_ref, held = refs[:-3], refs[-3], refs[-2], refs[-1]
    rows, channels, cols = turned_ref.shape
    pieces = [(b.at[e], (at_ref[2] ^ d) * size + e) for d, b in enumerate(blocks) for e in range(size)]
    total = jnp.zeros((rows, cols), jnp.float32)
    for piece, _ in pieces:
        total = total + piece[...].astype(jnp.float32)
    average = total * (1.0 / channels)
    spread = jnp.zeros((rows, cols), jnp.float32)
    for piece, c in pieces:
        value = piece[...].astype(jnp.float32)
        centred = value - average
        spread = spread + centred * centred
        for j in range(held.shape[0]):
            held[j, pl.ds(pl.multiple_of(c * rows, rows), rows), :] = value[:, j * LANES:(j + 1) * LANES]
    stats_ref[0] = average
    stats_ref[1] = spread
    for i in range(rows):
        for j in range(held.shape[0]):
            turned_ref[i, :, j * LANES:(j + 1) * LANES] = held[j, pl.ds(i, channels, stride=rows), :].astype(jnp.bfloat16)


def gather(blocks, at):
    size, rows, cols = blocks[0].shape
    channels = size * len(blocks)
    return pl.pallas_call(
        functools.partial(gather_kernel, size),
        grid=(rows // ROWS,),
        in_specs=[SMEM] + [pl.BlockSpec((size, ROWS, cols), lambda r: (0, r, 0))] * len(blocks),
        out_specs=[
            pl.BlockSpec((ROWS, channels, cols), lambda r: (r, 0, 0)),
            pl.BlockSpec((2, ROWS, cols), lambda r: (0, r, 0)),
        ],
        out_shape=[
            jax.ShapeDtypeStruct((rows, channels, cols), jnp.bfloat16),
            jax.ShapeDtypeStruct((2, rows, cols), jnp.float32),
        ],
        scratch_shapes=[pltpu.VMEM((cols // LANES, channels * ROWS, LANES), jnp.float32)],
        compiler_params=params(),
        cost_estimate=pl.CostEstimate(
            flops=4 * channels * rows * cols, bytes_accessed=4 * channels * rows * cols, transcendentals=0
        ),
        name="gather",
    )(at, *blocks)


def finish_kernel(gain_ref, column_ref, gate_ref, proj_ref, turned_ref, stats_ref, last_ref, out_ref, held, row_stats, gain_all):
    rows, early, cols = turned_ref.shape
    owners, size = last_ref.shape[:2]
    late = owners * size
    channels = early + late

    @pl.when(pl.program_id(0) == 0)
    def _():
        gain = jnp.broadcast_to(column_ref[...], (channels, channels)).T
        gain_all[...] = jnp.broadcast_to(gain[:, :1], gain_all.shape)

    total = stats_ref[0] * float(early)
    for o in range(owners):
        for e in range(size):
            total = total + last_ref[o, e].astype(jnp.float32)
    average = total * (1.0 / channels)
    shift = stats_ref[0] - average
    spread = stats_ref[1] + shift * shift * float(early)
    for o in range(owners):
        for e in range(size):
            centred = last_ref[o, e].astype(jnp.float32) - average
            spread = spread + centred * centred
    scale = lax.rsqrt(spread * (1.0 / channels) + norm_eps)
    row_stats[0] = average
    row_stats[1] = scale
    for o in range(owners):
        for e in range(size):
            c = o * size + e
            mixed = (last_ref[o, e].astype(jnp.float32) - average) * scale * gain_ref[early + c]
            for j in range(held.shape[0]):
                held[j, c * rows:(c + 1) * rows, :] = mixed[:, j * LANES:(j + 1) * LANES]

    def one_row(i, _):
        before = turned_ref[i].astype(jnp.float32) - row_stats[0, pl.ds(i, 1), :]
        before = before * row_stats[1, pl.ds(i, 1), :] * gain_all[:early]
        after_it = jnp.concatenate([held[j, pl.ds(i, late, stride=rows), :] for j in range(held.shape[0])], axis=1)
        mixed = jnp.concatenate([before.astype(jnp.bfloat16), after_it.astype(jnp.bfloat16)], axis=0)
        linear = lax.dot_general(mixed, proj_ref[...], (((0,), (0,)), ((), ())), preferred_element_type=jnp.float32)
        out_ref[i] = (gate_ref[i] * linear).astype(jnp.bfloat16)
        return 0

    lax.fori_loop(0, rows, one_row, 0, unroll=rows)


def finish(turned, stats, last, gate, gain, proj):
    rows, early, cols = turned.shape
    owners, size = last.shape[:2]
    channels = early + owners * size
    width = gate.shape[2]
    pair = pl.BlockSpec((ROWS, cols, width), lambda r: (r, 0, 0))
    return pl.pallas_call(
        finish_kernel,
        grid=(rows // ROWS,),
        in_specs=[
            SMEM,
            spec_whole((1, channels)),
            pair,
            spec_whole(proj.shape),
            pl.BlockSpec((ROWS, early, cols), lambda r: (r, 0, 0)),
            pl.BlockSpec((2, ROWS, cols), lambda r: (0, r, 0)),
            pl.BlockSpec((owners, size, ROWS, cols), lambda r: (0, 0, r, 0)),
        ],
        out_specs=pair,
        out_shape=jax.ShapeDtypeStruct((rows, cols, width), jnp.bfloat16),
        scratch_shapes=[
            pltpu.VMEM((cols // LANES, owners * size * ROWS, LANES), jnp.float32),
            pltpu.VMEM((2, ROWS, cols), jnp.float32),
            pltpu.VMEM((channels, cols), jnp.float32),
        ],
        compiler_params=params(),
        name="finish",
    )(gain, gain[None], gate, proj, turned, stats, last)


def exchange(x, axes):
    return lax.all_to_all(x, axes, split_axis=0, concat_axis=0, tiled=True)


def partners(blocks):
    n = len(blocks)
    moved = [blocks[0]]
    for d in range(1, n):
        block = blocks[d] if d <= 5 else after(blocks[d], moved[d - 5])
        moved.append(lax.ppermute(block, HALF, [(i, i ^ d) for i in range(n)]))
    return moved


def after(x, *others):
    return lax.optimization_barrier((x, *others))[0]


def per_device(
    pair_input, token_mask, norm_gain, left_gate, left_value, right_gate, right_value, sum_gain, out_gate, out_proj
):
    rows, cols, _ = pair_input.shape
    hidden = left_gate.shape[1]
    owners = lax.axis_size(HALF)
    chip = lax.axis_index(("half", "near", "y", "x"))
    at = jnp.stack([chip * rows, lax.axis_index("core"), lax.axis_index(HALF)]).astype(jnp.int32)
    col_mask = token_mask.reshape(-1, 1, cols)
    own = hidden // owners
    share = own // sum(SPLIT)
    sizes = tuple(s * share for s in SPLIT)
    firsts = tuple(sum(sizes[:q]) for q in range(len(sizes)))

    def right_chunk(x, q, norm_first):
        return project(
            x, right_gate, right_value, norm_gain, token_mask, None, at,
            firsts[q] * owners, (firsts[q] + sizes[q]) * owners, norm_first, None,
            functools.partial(write_right, sizes[q], owners), [(2 * owners, sizes[q])],
        )

    (right,) = right_chunk(pair_input, 0, True)
    first = exchange(right, ALL)
    normed, *lefts = project(
        pair_input, left_gate, left_value, norm_gain, token_mask, col_mask, at, 0, hidden, True, True,
        functools.partial(write_left, sizes, owners), [(own,)] * owners,
    )
    lefts = partners(lefts)
    (right,) = right_chunk(normed, 1, False)
    second = exchange(after(right, first, *lefts), ALL)
    blocks = partners(contract(lefts, first, at, 0, True))
    (out,) = contract(lefts, after(second, *blocks), at, firsts[1], False)
    last = exchange(out, HALF)
    gate = output_gate(normed, out_gate)
    turned, stats = gather(blocks, at)
    return finish(turned, stats, last, gate, sum_gain, out_proj)


def solution(mesh):
    grid = mesh.devices
    fine = Mesh(
        grid.reshape(grid.shape[0], 2, grid.shape[1] // 8, 2, 2, grid.shape[2]), ("groups", *ALL)
    )
    pair = P(("groups", "half", "near", "y", "x"), "core", None)
    return jax.shard_map(
        per_device, mesh=fine, in_specs=(pair, P("groups")) + (P(),) * 8, out_specs=pair, check_vma=False
    )
```

```python
import functools

import jax
import jax.numpy as jnp
from jax import lax
from jax.experimental import pallas as pl
from jax.experimental.pallas import tpu as pltpu
from jax.sharding import Mesh
from jax.sharding import PartitionSpec as P

norm_eps = 1e-05
ROWS = 16
LANES = 128
VMEM_BYTES = 63 * 1024 * 1024 + 256 * 1024
HALF = ("near", "y", "x", "core")
ALL = ("half", *HALF)
SPLIT = (5, 3)


def params(vmem=VMEM_BYTES):
    return pltpu.CompilerParams(vmem_limit_bytes=vmem)


def sigmoid(x):
    grown = 1.0 + jnp.exp(-jnp.maximum(x, -80.0))
    guess = pl.reciprocal(grown, approx=True)
    return guess * (2.0 - grown * guess)


def spec_whole(shape):
    return pl.BlockSpec(shape, lambda r: (0,) * len(shape))


SMEM = pl.BlockSpec(memory_space=pltpu.SMEM)


def project_kernel(low, high, norm_first, keep, write, mask_ref, at_ref, x_ref, gate_ref, value_ref, gain_ref, *refs):
    *outs, held, w_ref, gain_all = refs
    col_valid = 1.0
    if keep is not None:
        col_ref, *outs = outs
        col_valid = col_ref[at_ref[1]].astype(jnp.float32)
    count = high - low
    step = pl.program_id(0)

    @pl.when(step == 0)
    def _():
        w_ref[:count] = gate_ref[...].astype(jnp.float32).T[low:high].astype(jnp.bfloat16)
        w_ref[count:] = value_ref[...].astype(jnp.float32).T[low:high].astype(jnp.bfloat16)
        gain = jnp.broadcast_to(gain_ref[...], (gain_ref.shape[1], gain_ref.shape[1])).T
        gain_all[...] = jnp.broadcast_to(gain[:, :1], gain_all.shape)

    first_row = at_ref[0] + step * ROWS
    if keep:
        normed_ref, *outs = outs

    def one_row(i, _):
        if norm_first:
            x = x_ref[i].T.astype(jnp.float32)
            centred = x - jnp.mean(x, axis=0, keepdims=True)
            spread = jnp.mean(centred * centred, axis=0, keepdims=True)
            normed = (centred * lax.rsqrt(spread + norm_eps) * gain_all[...]).astype(jnp.bfloat16)
            if keep:
                normed_ref[i] = normed
        else:
            normed = x_ref[i]
        both = jnp.dot(w_ref[...], normed, preferred_element_type=jnp.float32)
        valid = mask_ref[first_row + i].astype(jnp.float32) * col_valid
        gated = sigmoid(both[:count]) * both[count:] * valid
        for j in range(held.shape[0]):
            held[j, pl.ds(pl.multiple_of(i * count, 8), count), :] = gated[:, j * LANES:(j + 1) * LANES]
        return 0

    lax.fori_loop(0, ROWS, one_row, 0, unroll=ROWS)

    def channel(j, c):
        return held[j, pl.ds(c, ROWS, stride=count), :].astype(jnp.bfloat16)

    write(outs, channel, at_ref)


def write_right(size, owners, outs, channel, at_ref):
    (out,) = outs

    def one_owner(o, _):
        for e in range(size):
            for j in range(out.shape[-1] // LANES):
                block = channel(j, o * size + e)
                for h in range(2):
                    out[h * owners + o, e, :, j * LANES:(j + 1) * LANES] = block
        return 0

    lax.fori_loop(0, owners, one_owner, 0, unroll=2)


def write_left(sizes, owners, outs, channel, at_ref):
    for d, out in enumerate(outs):
        owner = at_ref[2] ^ d
        first = 0
        for size in sizes:
            for e in range(size):
                for j in range(out.shape[-1] // LANES):
                    out[first + e, :, j * LANES:(j + 1) * LANES] = channel(j, first * owners + owner * size + e)
            first += size


def project(x, gate, value, gain, mask, col_mask, at, low, high, norm_first, keep, write, out_blocks):
    rows, cols, width = x.shape if norm_first else (x.shape[0], x.shape[2], x.shape[1])
    count = high - low
    x_spec = pl.BlockSpec((ROWS, *x.shape[1:]), lambda r: (r, 0, 0))
    out_shape = [jax.ShapeDtypeStruct((*lead, rows, cols), jnp.bfloat16) for lead in out_blocks]
    out_specs = [pl.BlockSpec((*lead, ROWS, cols), lambda r, n=len(lead): (0,) * n + (r, 0)) for lead in out_blocks]
    if keep:
        out_shape = [jax.ShapeDtypeStruct((rows, width, cols), jnp.bfloat16), *out_shape]
        out_specs = [pl.BlockSpec((ROWS, width, cols), lambda r: (r, 0, 0)), *out_specs]
    extra = [] if keep is None else [col_mask]
    return pl.pallas_call(
        functools.partial(project_kernel, low, high, norm_first, keep, write),
        grid=(rows // ROWS,),
        in_specs=[SMEM, SMEM, x_spec]
        + [spec_whole(gate.shape)] * 2 + [spec_whole((1, width))] + [spec_whole(e.shape) for e in extra],
        out_specs=out_specs,
        out_shape=out_shape,
        scratch_shapes=[
            pltpu.VMEM((cols // LANES, ROWS * count, LANES), jnp.float32),
            pltpu.VMEM((2 * count, width), jnp.bfloat16),
            pltpu.VMEM((width, cols), jnp.float32),
        ],
        compiler_params=params(),
        cost_estimate=pl.CostEstimate(
            flops=4 * rows * cols * width * count, bytes_accessed=8 * rows * cols * width, transcendentals=rows * cols * count
        ),
        name="project",
    )(mask, at, x, gate, value, gain[None], *extra)


def gate_kernel(normed_ref, gate_ref, out_ref):
    def one_row(i, _):
        gate = lax.dot_general(normed_ref[i], gate_ref[...], (((0,), (0,)), ((), ())), preferred_element_type=jnp.float32)
        out_ref[i] = sigmoid(gate).astype(out_ref.dtype)
        return 0

    lax.fori_loop(0, normed_ref.shape[0], one_row, 0, unroll=4)


def output_gate(normed, out_gate):
    rows, width, cols = normed.shape
    return pl.pallas_call(
        gate_kernel,
        grid=(rows // ROWS,),
        in_specs=[pl.BlockSpec((ROWS, width, cols), lambda r: (r, 0, 0)), spec_whole(out_gate.shape)],
        out_specs=pl.BlockSpec((ROWS, cols, width), lambda r: (r, 0, 0)),
        out_shape=jax.ShapeDtypeStruct((rows, cols, width), jnp.bfloat16),
        compiler_params=params(),
        cost_estimate=pl.CostEstimate(
            flops=2 * rows * cols * width * width, bytes_accessed=4 * rows * cols * width, transcendentals=rows * cols * width
        ),
        name="output_gate",
    )(normed, out_gate)


def contract_kernel(n, by_partner, rows, cols, at_ref, *refs):
    lefts, right = refs[:n], refs[n]
    outs = refs[n + 1:-3]
    left_all, right_all, sums = refs[-3:]
    for s in range(right.shape[0]):
        right_all[s % 2, (s // 2) * rows:(s // 2 + 1) * rows, :] = right[s, 0]
    for d, left in enumerate(lefts):
        source = at_ref[2] ^ d
        left_all[source & 1, pl.ds(pl.multiple_of((source >> 1) * rows, rows), rows), :] = left[0]
    dims = (((1,), (1,)), ((), ()))
    for k in range(2):
        total = sum(
            lax.dot_general(left_all[p], right_all[p, k * cols:(k + 1) * cols, :], dims, preferred_element_type=jnp.float32)
            for p in range(2)
        ).astype(jnp.bfloat16)
        if by_partner:
            sums[k] = total
        else:
            for b in range(n // 2):
                outs[0][2 * b + k, 0] = total[b * rows:(b + 1) * rows]
    if by_partner:
        for d, out in enumerate(outs):
            target = at_ref[2] ^ d
            out[0] = sums[target & 1, pl.ds(pl.multiple_of((target >> 1) * rows, rows), rows), :]


def contract(lefts, right, at, first, by_partner):
    everyone, size, rows, cols = right.shape
    n = len(lefts)
    out_shape = [jax.ShapeDtypeStruct((size, rows, cols), jnp.bfloat16)] * n
    out_specs = [pl.BlockSpec((1, rows, cols), lambda q: (q, 0, 0))] * n
    if not by_partner:
        out_shape = [jax.ShapeDtypeStruct((n, size, rows, cols), jnp.bfloat16)]
        out_specs = [pl.BlockSpec((n, 1, rows, cols), lambda q: (0, q, 0, 0))]
    return pl.pallas_call(
        functools.partial(contract_kernel, n, by_partner, rows, cols),
        grid=(size,),
        in_specs=[SMEM]
        + [pl.BlockSpec((1, rows, cols), lambda q: (first + q, 0, 0))] * n
        + [pl.BlockSpec((everyone, 1, rows, cols), lambda q: (0, q, 0, 0))],
        out_specs=out_specs,
        out_shape=out_shape,
        scratch_shapes=[
            pltpu.VMEM((2, n // 2 * rows, cols), jnp.bfloat16),
            pltpu.VMEM((2, everyone // 2 * rows, cols), jnp.bfloat16),
            pltpu.VMEM((2, n // 2 * rows, cols), jnp.bfloat16),
        ],
        compiler_params=params(),
        cost_estimate=pl.CostEstimate(
            flops=size * 2 * n * n * everyone // 4 * rows * rows * cols,
            bytes_accessed=size * (everyone + 2 * n) * rows * cols * 2,
            transcendentals=0,
        ),
        name="contract",
    )(at, *lefts, right)


def gather_kernel(size, at_ref, *refs):
    blocks, turned_ref, stats_ref, held = refs[:-3], refs[-3], refs[-2], refs[-1]
    rows, channels, cols = turned_ref.shape
    pieces = [(b.at[e], (at_ref[2] ^ d) * size + e) for d, b in enumerate(blocks) for e in range(size)]
    total = jnp.zeros((rows, cols), jnp.float32)
    for piece, _ in pieces:
        total = total + piece[...].astype(jnp.float32)
    average = total * (1.0 / channels)
    spread = jnp.zeros((rows, cols), jnp.float32)
    for piece, c in pieces:
        value = piece[...].astype(jnp.float32)
        centred = value - average
        spread = spread + centred * centred
        for j in range(held.shape[0]):
            held[j, pl.ds(pl.multiple_of(c * rows, rows), rows), :] = value[:, j * LANES:(j + 1) * LANES]
    stats_ref[0] = average
    stats_ref[1] = spread
    for i in range(rows):
        for j in range(held.shape[0]):
            turned_ref[i, :, j * LANES:(j + 1) * LANES] = held[j, pl.ds(i, channels, stride=rows), :].astype(jnp.bfloat16)


def gather(blocks, at):
    size, rows, cols = blocks[0].shape
    channels = size * len(blocks)
    return pl.pallas_call(
        functools.partial(gather_kernel, size),
        grid=(rows // ROWS,),
        in_specs=[SMEM] + [pl.BlockSpec((size, ROWS, cols), lambda r: (0, r, 0))] * len(blocks),
        out_specs=[
            pl.BlockSpec((ROWS, channels, cols), lambda r: (r, 0, 0)),
            pl.BlockSpec((2, ROWS, cols), lambda r: (0, r, 0)),
        ],
        out_shape=[
            jax.ShapeDtypeStruct((rows, channels, cols), jnp.bfloat16),
            jax.ShapeDtypeStruct((2, rows, cols), jnp.float32),
        ],
        scratch_shapes=[pltpu.VMEM((cols // LANES, channels * ROWS, LANES), jnp.float32)],
        compiler_params=params(),
        cost_estimate=pl.CostEstimate(
            flops=4 * channels * rows * cols, bytes_accessed=4 * channels * rows * cols, transcendentals=0
        ),
        name="gather",
    )(at, *blocks)


def finish_kernel(gain_ref, column_ref, gate_ref, proj_ref, turned_ref, stats_ref, last_ref, out_ref, held, row_stats, gain_all):
    rows, early, cols = turned_ref.shape
    owners, size = last_ref.shape[:2]
    late = owners * size
    channels = early + late

    @pl.when(pl.program_id(0) == 0)
    def _():
        gain = jnp.broadcast_to(column_ref[...], (channels, channels)).T
        gain_all[...] = jnp.broadcast_to(gain[:, :1], gain_all.shape)

    total = stats_ref[0] * float(early)
    for o in range(owners):
        for e in range(size):
            total = total + last_ref[o, e].astype(jnp.float32)
    average = total * (1.0 / channels)
    shift = stats_ref[0] - average
    spread = stats_ref[1] + shift * shift * float(early)
    for o in range(owners):
        for e in range(size):
            centred = last_ref[o, e].astype(jnp.float32) - average
            spread = spread + centred * centred
    scale = lax.rsqrt(spread * (1.0 / channels) + norm_eps)
    row_stats[0] = average
    row_stats[1] = scale
    for o in range(owners):
        for e in range(size):
            c = o * size + e
            mixed = (last_ref[o, e].astype(jnp.float32) - average) * scale * gain_ref[early + c]
            for j in range(held.shape[0]):
                held[j, c * rows:(c + 1) * rows, :] = mixed[:, j * LANES:(j + 1) * LANES]

    def one_row(i, _):
        before = turned_ref[i].astype(jnp.float32) - row_stats[0, pl.ds(i, 1), :]
        before = before * row_stats[1, pl.ds(i, 1), :] * gain_all[:early]
        after_it = jnp.concatenate([held[j, pl.ds(i, late, stride=rows), :] for j in range(held.shape[0])], axis=1)
        mixed = jnp.concatenate([before.astype(jnp.bfloat16), after_it.astype(jnp.bfloat16)], axis=0)
        linear = lax.dot_general(mixed, proj_ref[...], (((0,), (0,)), ((), ())), preferred_element_type=jnp.float32)
        out_ref[i] = (gate_ref[i].astype(jnp.float32) * linear).astype(jnp.bfloat16)
        return 0

    lax.fori_loop(0, rows, one_row, 0, unroll=rows)


def finish(turned, stats, last, gate, gain, proj):
    rows, early, cols = turned.shape
    owners, size = last.shape[:2]
    channels = early + owners * size
    width = gate.shape[2]
    pair = pl.BlockSpec((ROWS, cols, width), lambda r: (r, 0, 0))
    return pl.pallas_call(
        finish_kernel,
        grid=(rows // ROWS,),
        in_specs=[
            SMEM,
            spec_whole((1, channels)),
            pair,
            spec_whole(proj.shape),
            pl.BlockSpec((ROWS, early, cols), lambda r: (r, 0, 0)),
            pl.BlockSpec((2, ROWS, cols), lambda r: (0, r, 0)),
            pl.BlockSpec((owners, size, ROWS, cols), lambda r: (0, 0, r, 0)),
        ],
        out_specs=pair,
        out_shape=jax.ShapeDtypeStruct((rows, cols, width), jnp.bfloat16),
        scratch_shapes=[
            pltpu.VMEM((cols // LANES, owners * size * ROWS, LANES), jnp.float32),
            pltpu.VMEM((2, ROWS, cols), jnp.float32),
            pltpu.VMEM((channels, cols), jnp.float32),
        ],
        compiler_params=params(),
        name="finish",
    )(gain, gain[None], gate, proj, turned, stats, last)


def exchange(x, axes):
    return lax.all_to_all(x, axes, split_axis=0, concat_axis=0, tiled=True)


def partners(blocks, abreast):
    n = len(blocks)
    moved = [blocks[0]]
    for d in range(1, n):
        block = blocks[d] if d <= abreast else after(blocks[d], moved[d - abreast])
        moved.append(lax.ppermute(block, HALF, [(i, i ^ d) for i in range(n)]))
    return moved


def after(x, *others):
    return lax.optimization_barrier((x, *others))[0]


def per_device(
    pair_input, token_mask, norm_gain, left_gate, left_value, right_gate, right_value, sum_gain, out_gate, out_proj
):
    rows, cols, _ = pair_input.shape
    hidden = left_gate.shape[1]
    owners = lax.axis_size(HALF)
    chip = lax.axis_index(("half", "near", "y", "x"))
    at = jnp.stack([chip * rows, lax.axis_index("core"), lax.axis_index(HALF)]).astype(jnp.int32)
    col_mask = token_mask.reshape(-1, 1, cols)
    own = hidden // owners
    share = own // sum(SPLIT)
    sizes = tuple(s * share for s in SPLIT)
    firsts = tuple(sum(sizes[:q]) for q in range(len(sizes)))

    def right_chunk(x, q, norm_first):
        return project(
            x, right_gate, right_value, norm_gain, token_mask, None, at,
            firsts[q] * owners, (firsts[q] + sizes[q]) * owners, norm_first, None,
            functools.partial(write_right, sizes[q], owners), [(2 * owners, sizes[q])],
        )

    (right,) = right_chunk(pair_input, 0, True)
    first = exchange(right, ALL)
    normed, *lefts = project(
        pair_input, left_gate, left_value, norm_gain, token_mask, col_mask, at, 0, hidden, True, True,
        functools.partial(write_left, sizes, owners), [(own,)] * owners,
    )
    lefts = partners(lefts, 6)
    (right,) = right_chunk(normed, 1, False)
    second = exchange(after(right, first, *lefts), ALL)
    blocks = partners(contract(lefts, first, at, 0, True), 5)
    (out,) = contract(lefts, after(second, *blocks), at, firsts[1], False)
    last = exchange(out, HALF)
    gate = output_gate(normed, out_gate)
    turned, stats = gather(blocks, at)
    return finish(turned, stats, last, gate, sum_gain, out_proj)


def solution(mesh):
    grid = mesh.devices
    fine = Mesh(
        grid.reshape(grid.shape[0], 2, grid.shape[1] // 8, 2, 2, grid.shape[2]), ("groups", *ALL)
    )
    pair = P(("groups", "half", "near", "y", "x"), "core", None)
    return jax.shard_map(
        per_device, mesh=fine, in_specs=(pair, P("groups")) + (P(),) * 8, out_specs=pair, check_vma=False
    )
```

```python
import functools

import jax
import jax.numpy as jnp
from jax import lax
from jax.experimental import pallas as pl
from jax.experimental.pallas import tpu as pltpu
from jax.sharding import Mesh
from jax.sharding import PartitionSpec as P

norm_eps = 1e-05
ROWS = 16
LANES = 128
VMEM_BYTES = 63 * 1024 * 1024 + 256 * 1024
HALF = ("near", "y", "x", "core")
ALL = ("half", *HALF)
SPLIT = (5, 3)


def params(vmem=VMEM_BYTES):
    return pltpu.CompilerParams(vmem_limit_bytes=vmem)


def sigmoid(x):
    grown = 1.0 + jnp.exp(-jnp.maximum(x, -80.0))
    guess = pl.reciprocal(grown, approx=True)
    return guess * (2.0 - grown * guess)


def spec_whole(shape):
    return pl.BlockSpec(shape, lambda r: (0,) * len(shape))


SMEM = pl.BlockSpec(memory_space=pltpu.SMEM)


def project_kernel(low, high, norm_first, keep, write, mask_ref, at_ref, x_ref, gate_ref, value_ref, gain_ref, *refs):
    *outs, held, w_ref, gain_all = refs
    col_valid = 1.0
    if keep is not None:
        col_ref, *outs = outs
        col_valid = col_ref[at_ref[1]].astype(jnp.float32)
    count = high - low
    step = pl.program_id(0)

    @pl.when(step == 0)
    def _():
        w_ref[:count] = gate_ref[...].astype(jnp.float32).T[low:high].astype(jnp.bfloat16)
        w_ref[count:] = value_ref[...].astype(jnp.float32).T[low:high].astype(jnp.bfloat16)
        gain = jnp.broadcast_to(gain_ref[...], (gain_ref.shape[1], gain_ref.shape[1])).T
        gain_all[...] = jnp.broadcast_to(gain[:, :1], gain_all.shape)

    first_row = (lax.axis_index(("half", "near", "y", "x")) * x_ref.shape[0] * pl.num_programs(0)) + step * ROWS
    if keep:
        normed_ref, *outs = outs

    def one_row(i, _):
        if norm_first:
            x = x_ref[i].T.astype(jnp.float32)
            centred = x - jnp.mean(x, axis=0, keepdims=True)
            spread = jnp.mean(centred * centred, axis=0, keepdims=True)
            normed = (centred * lax.rsqrt(spread + norm_eps) * gain_all[...]).astype(jnp.bfloat16)
            if keep:
                normed_ref[i] = normed
        else:
            normed = x_ref[i]
        both = jnp.dot(w_ref[...], normed, preferred_element_type=jnp.float32)
        valid = mask_ref[first_row + i].astype(jnp.float32) * col_valid
        gated = sigmoid(both[:count]) * both[count:] * valid
        for j in range(held.shape[0]):
            held[j, pl.ds(pl.multiple_of(i * count, 8), count), :] = gated[:, j * LANES:(j + 1) * LANES]
        return 0

    lax.fori_loop(0, ROWS, one_row, 0, unroll=ROWS)

    def channel(j, c):
        return held[j, pl.ds(c, ROWS, stride=count), :].astype(jnp.bfloat16)

    write(outs, channel, at_ref)


def write_right(size, owners, outs, channel, at_ref):
    (out,) = outs

    def one_owner(o, _):
        for e in range(size):
            for j in range(out.shape[-1] // LANES):
                block = channel(j, o * size + e)
                for h in range(2):
                    out[h * owners + o, e, :, j * LANES:(j + 1) * LANES] = block
        return 0

    lax.fori_loop(0, owners, one_owner, 0, unroll=2)


def write_left(sizes, owners, outs, channel, at_ref):
    for d, out in enumerate(outs):
        owner = at_ref[2] ^ d
        first = 0
        for size in sizes:
            for e in range(size):
                for j in range(out.shape[-1] // LANES):
                    out[first + e, :, j * LANES:(j + 1) * LANES] = channel(j, first * owners + owner * size + e)
            first += size


def project(x, gate, value, gain, mask, col_mask, at, low, high, norm_first, keep, write, out_blocks):
    rows, cols, width = x.shape if norm_first else (x.shape[0], x.shape[2], x.shape[1])
    count = high - low
    x_spec = pl.BlockSpec((ROWS, *x.shape[1:]), lambda r: (r, 0, 0))
    out_shape = [jax.ShapeDtypeStruct((*lead, rows, cols), jnp.bfloat16) for lead in out_blocks]
    out_specs = [pl.BlockSpec((*lead, ROWS, cols), lambda r, n=len(lead): (0,) * n + (r, 0)) for lead in out_blocks]
    if keep:
        out_shape = [jax.ShapeDtypeStruct((rows, width, cols), jnp.bfloat16), *out_shape]
        out_specs = [pl.BlockSpec((ROWS, width, cols), lambda r: (r, 0, 0)), *out_specs]
    extra = [] if keep is None else [col_mask]
    return pl.pallas_call(
        functools.partial(project_kernel, low, high, norm_first, keep, write),
        grid=(rows // ROWS,),
        in_specs=[SMEM, SMEM, x_spec]
        + [spec_whole(gate.shape)] * 2 + [spec_whole((1, width))] + [spec_whole(e.shape) for e in extra],
        out_specs=out_specs,
        out_shape=out_shape,
        scratch_shapes=[
            pltpu.VMEM((cols // LANES, ROWS * count, LANES), jnp.float32),
            pltpu.VMEM((2 * count, width), jnp.bfloat16),
            pltpu.VMEM((width, cols), jnp.float32),
        ],
        compiler_params=params(),
        cost_estimate=pl.CostEstimate(
            flops=4 * rows * cols * width * count, bytes_accessed=8 * rows * cols * width, transcendentals=rows * cols * count
        ),
        name="project",
    )(mask, mask if at is None else at, x, gate, value, gain[None], *extra)


def gate_kernel(normed_ref, gate_ref, out_ref):
    def one_row(i, _):
        gate = lax.dot_general(normed_ref[i], gate_ref[...], (((0,), (0,)), ((), ())), preferred_element_type=jnp.float32)
        out_ref[i] = sigmoid(gate).astype(out_ref.dtype)
        return 0

    lax.fori_loop(0, normed_ref.shape[0], one_row, 0, unroll=4)


def output_gate(normed, out_gate):
    rows, width, cols = normed.shape
    return pl.pallas_call(
        gate_kernel,
        grid=(rows // ROWS,),
        in_specs=[pl.BlockSpec((ROWS, width, cols), lambda r: (r, 0, 0)), spec_whole(out_gate.shape)],
        out_specs=pl.BlockSpec((ROWS, cols, width), lambda r: (r, 0, 0)),
        out_shape=jax.ShapeDtypeStruct((rows, cols, width), jnp.bfloat16),
        compiler_params=params(),
        cost_estimate=pl.CostEstimate(
            flops=2 * rows * cols * width * width, bytes_accessed=4 * rows * cols * width, transcendentals=rows * cols * width
        ),
        name="output_gate",
    )(normed, out_gate)


def contract_kernel(n, by_partner, rows, cols, at_ref, *refs):
    lefts, right = refs[:n], refs[n]
    outs = refs[n + 1:-3]
    left_all, right_all, sums = refs[-3:]
    for s in range(right.shape[0]):
        right_all[s % 2, (s // 2) * rows:(s // 2 + 1) * rows, :] = right[s, 0]
    for d, left in enumerate(lefts):
        source = at_ref[2] ^ d
        left_all[source & 1, pl.ds(pl.multiple_of((source >> 1) * rows, rows), rows), :] = left[0]
    dims = (((1,), (1,)), ((), ()))
    for k in range(2):
        total = sum(
            lax.dot_general(left_all[p], right_all[p, k * cols:(k + 1) * cols, :], dims, preferred_element_type=jnp.float32)
            for p in range(2)
        ).astype(jnp.bfloat16)
        if by_partner:
            sums[k] = total
        else:
            for b in range(n // 2):
                outs[0][2 * b + k, 0] = total[b * rows:(b + 1) * rows]
    if by_partner:
        for d, out in enumerate(outs):
            target = at_ref[2] ^ d
            out[0] = sums[target & 1, pl.ds(pl.multiple_of((target >> 1) * rows, rows), rows), :]


def contract(lefts, right, at, first, by_partner):
    everyone, size, rows, cols = right.shape
    n = len(lefts)
    out_shape = [jax.ShapeDtypeStruct((size, rows, cols), jnp.bfloat16)] * n
    out_specs = [pl.BlockSpec((1, rows, cols), lambda q: (q, 0, 0))] * n
    if not by_partner:
        out_shape = [jax.ShapeDtypeStruct((n, size, rows, cols), jnp.bfloat16)]
        out_specs = [pl.BlockSpec((n, 1, rows, cols), lambda q: (0, q, 0, 0))]
    return pl.pallas_call(
        functools.partial(contract_kernel, n, by_partner, rows, cols),
        grid=(size,),
        in_specs=[SMEM]
        + [pl.BlockSpec((1, rows, cols), lambda q: (first + q, 0, 0))] * n
        + [pl.BlockSpec((everyone, 1, rows, cols), lambda q: (0, q, 0, 0))],
        out_specs=out_specs,
        out_shape=out_shape,
        scratch_shapes=[
            pltpu.VMEM((2, n // 2 * rows, cols), jnp.bfloat16),
            pltpu.VMEM((2, everyone // 2 * rows, cols), jnp.bfloat16),
            pltpu.VMEM((2, n // 2 * rows, cols), jnp.bfloat16),
        ],
        compiler_params=params(),
        cost_estimate=pl.CostEstimate(
            flops=size * 2 * n * n * everyone // 4 * rows * rows * cols,
            bytes_accessed=size * (everyone + 2 * n) * rows * cols * 2,
            transcendentals=0,
        ),
        name="contract",
    )(at, *lefts, right)


def gather_kernel(size, at_ref, *refs):
    blocks, turned_ref, stats_ref, held = refs[:-3], refs[-3], refs[-2], refs[-1]
    rows, channels, cols = turned_ref.shape
    pieces = [(b.at[e], (at_ref[2] ^ d) * size + e) for d, b in enumerate(blocks) for e in range(size)]
    total = jnp.zeros((rows, cols), jnp.float32)
    for piece, _ in pieces:
        total = total + piece[...].astype(jnp.float32)
    average = total * (1.0 / channels)
    spread = jnp.zeros((rows, cols), jnp.float32)
    for piece, c in pieces:
        value = piece[...].astype(jnp.float32)
        centred = value - average
        spread = spread + centred * centred
        for j in range(held.shape[0]):
            held[j, pl.ds(pl.multiple_of(c * rows, rows), rows), :] = value[:, j * LANES:(j + 1) * LANES]
    stats_ref[0] = average
    stats_ref[1] = spread
    for i in range(rows):
        for j in range(held.shape[0]):
            turned_ref[i, :, j * LANES:(j + 1) * LANES] = held[j, pl.ds(i, channels, stride=rows), :].astype(jnp.bfloat16)


def gather(blocks, at):
    size, rows, cols = blocks[0].shape
    channels = size * len(blocks)
    return pl.pallas_call(
        functools.partial(gather_kernel, size),
        grid=(rows // ROWS,),
        in_specs=[SMEM] + [pl.BlockSpec((size, ROWS, cols), lambda r: (0, r, 0))] * len(blocks),
        out_specs=[
            pl.BlockSpec((ROWS, channels, cols), lambda r: (r, 0, 0)),
            pl.BlockSpec((2, ROWS, cols), lambda r: (0, r, 0)),
        ],
        out_shape=[
            jax.ShapeDtypeStruct((rows, channels, cols), jnp.bfloat16),
            jax.ShapeDtypeStruct((2, rows, cols), jnp.float32),
        ],
        scratch_shapes=[pltpu.VMEM((cols // LANES, channels * ROWS, LANES), jnp.float32)],
        compiler_params=params(),
        cost_estimate=pl.CostEstimate(
            flops=4 * channels * rows * cols, bytes_accessed=4 * channels * rows * cols, transcendentals=0
        ),
        name="gather",
    )(at, *blocks)


def finish_kernel(gain_ref, column_ref, gate_ref, proj_ref, turned_ref, stats_ref, last_ref, out_ref, held, row_stats, gain_all):
    rows, early, cols = turned_ref.shape
    owners, size = last_ref.shape[:2]
    late = owners * size
    channels = early + late

    @pl.when(pl.program_id(0) == 0)
    def _():
        gain = jnp.broadcast_to(column_ref[...], (channels, channels)).T
        gain_all[...] = jnp.broadcast_to(gain[:, :1], gain_all.shape)

    total = stats_ref[0] * float(early)
    for o in range(owners):
        for e in range(size):
            total = total + last_ref[o, e].astype(jnp.float32)
    average = total * (1.0 / channels)
    shift = stats_ref[0] - average
    spread = stats_ref[1] + shift * shift * float(early)
    for o in range(owners):
        for e in range(size):
            centred = last_ref[o, e].astype(jnp.float32) - average
            spread = spread + centred * centred
    scale = lax.rsqrt(spread * (1.0 / channels) + norm_eps)
    row_stats[0] = average
    row_stats[1] = scale
    for o in range(owners):
        for e in range(size):
            c = o * size + e
            mixed = (last_ref[o, e].astype(jnp.float32) - average) * scale * gain_ref[early + c]
            for j in range(held.shape[0]):
                held[j, c * rows:(c + 1) * rows, :] = mixed[:, j * LANES:(j + 1) * LANES]

    def one_row(i, _):
        before = turned_ref[i].astype(jnp.float32) - row_stats[0, pl.ds(i, 1), :]
        before = before * row_stats[1, pl.ds(i, 1), :] * gain_all[:early]
        after_it = jnp.concatenate([held[j, pl.ds(i, late, stride=rows), :] for j in range(held.shape[0])], axis=1)
        mixed = jnp.concatenate([before.astype(jnp.bfloat16), after_it.astype(jnp.bfloat16)], axis=0)
        linear = lax.dot_general(mixed, proj_ref[...], (((0,), (0,)), ((), ())), preferred_element_type=jnp.float32)
        out_ref[i] = (gate_ref[i].astype(jnp.float32) * linear).astype(jnp.bfloat16)
        return 0

    lax.fori_loop(0, rows, one_row, 0, unroll=rows)


def finish(turned, stats, last, gate, gain, proj):
    rows, early, cols = turned.shape
    owners, size = last.shape[:2]
    channels = early + owners * size
    width = gate.shape[2]
    pair = pl.BlockSpec((ROWS, cols, width), lambda r: (r, 0, 0))
    return pl.pallas_call(
        finish_kernel,
        grid=(rows // ROWS,),
        in_specs=[
            SMEM,
            spec_whole((1, channels)),
            pair,
            spec_whole(proj.shape),
            pl.BlockSpec((ROWS, early, cols), lambda r: (r, 0, 0)),
            pl.BlockSpec((2, ROWS, cols), lambda r: (0, r, 0)),
            pl.BlockSpec((owners, size, ROWS, cols), lambda r: (0, 0, r, 0)),
        ],
        out_specs=pair,
        out_shape=jax.ShapeDtypeStruct((rows, cols, width), jnp.bfloat16),
        scratch_shapes=[
            pltpu.VMEM((cols // LANES, owners * size * ROWS, LANES), jnp.float32),
            pltpu.VMEM((2, ROWS, cols), jnp.float32),
            pltpu.VMEM((channels, cols), jnp.float32),
        ],
        compiler_params=params(),
        name="finish",
    )(gain, gain[None], gate, proj, turned, stats, last)


def exchange(x, axes):
    return lax.all_to_all(x, axes, split_axis=0, concat_axis=0, tiled=True)


def partners(blocks, abreast):
    n = len(blocks)
    moved = {0: blocks[0]}
    order = [*range(1, n // 2), *(d ^ 1 for d in range(n // 2, n))]
    for t, d in enumerate(order):
        block = blocks[d] if t < abreast else after(blocks[d], moved[order[t - abreast]])
        moved[d] = lax.ppermute(block, HALF, [(i, i ^ d) for i in range(n)])
    return [moved[d] for d in range(n)]


def after(x, *others):
    return lax.optimization_barrier((x, *others))[0]


def per_device(
    pair_input, token_mask, norm_gain, left_gate, left_value, right_gate, right_value, sum_gain, out_gate, out_proj
):
    rows, cols, _ = pair_input.shape
    hidden = left_gate.shape[1]
    owners = lax.axis_size(HALF)
    chip = lax.axis_index(("half", "near", "y", "x"))
    at = jnp.stack([chip * rows, lax.axis_index("core"), lax.axis_index(HALF)]).astype(jnp.int32)
    col_mask = token_mask.reshape(-1, 1, cols)
    own = hidden // owners
    share = own // sum(SPLIT)
    sizes = tuple(s * share for s in SPLIT)
    firsts = tuple(sum(sizes[:q]) for q in range(len(sizes)))

    def right_chunk(x, q, norm_first):
        return project(
            x, right_gate, right_value, norm_gain, token_mask, None, None,
            firsts[q] * owners, (firsts[q] + sizes[q]) * owners, norm_first, None,
            functools.partial(write_right, sizes[q], owners), [(2 * owners, sizes[q])],
        )

    (right,) = right_chunk(pair_input, 0, True)
    first = exchange(right, ALL)
    normed, *lefts = project(
        pair_input, left_gate, left_value, norm_gain, token_mask, col_mask, at, 0, hidden, True, True,
        functools.partial(write_left, sizes, owners), [(own,)] * owners,
    )
    lefts = partners(lefts, 6)
    (right,) = right_chunk(normed, 1, False)
    second = exchange(after(right, first, *lefts), ALL)
    blocks = partners(contract(lefts, first, at, 0, True), 5)
    (out,) = contract(lefts, after(second, *blocks), at, firsts[1], False)
    last = exchange(out, HALF)
    gate = output_gate(normed, out_gate)
    turned, stats = gather(blocks, at)
    return finish(turned, stats, last, gate, sum_gain, out_proj)


def solution(mesh):
    grid = mesh.devices
    fine = Mesh(
        grid.reshape(grid.shape[0], 2, grid.shape[1] // 8, 2, 2, grid.shape[2]), ("groups", *ALL)
    )
    pair = P(("groups", "half", "near", "y", "x"), "core", None)
    return jax.shard_map(
        per_device, mesh=fine, in_specs=(pair, P("groups")) + (P(),) * 8, out_specs=pair, check_vma=False
    )
```
